32 devices in a mesh: groups: 2 (over y), wide: 4 (over x, core), tp: 4 (over z).
Axes of the slice: x: 2, y: 2, z: 4, core: 2. Of those that a mesh axis runs over, the one named last changes fastest.
Arguments:
- queries: bfloat16 [256, 8192], P(('groups', 'wide'), 'tp'), parts along dimension 0, may hold values from -26 to 26
- cached_key_rows: bfloat16 [256, 8, 256, 128], P(('groups', 'wide'), 'tp'), parts along dimension 0, may hold values from -16 to 16
- cached_value_rows: bfloat16 [256, 8, 256, 128], P(('groups', 'wide'), 'tp'), parts along dimension 0, may hold values from -6 to 6
- fresh_token_key: bfloat16 [256, 1024], P(('groups', 'wide'), 'tp'), parts along dimension 0, may hold values from -6 to 6
- fresh_token_value: bfloat16 [256, 1024], P(('groups', 'wide'), 'tp'), parts along dimension 0, may hold values from -6 to 6
- lengths: int32 [256], P(('groups', 'wide')), parts along dimension 0, may hold values from 1 to 256, 16384 in all
- residual: bfloat16 [256, 8192], P(('groups', 'wide'), 'tp'), parts along dimension 0, may hold values from -13 to 13
- norm_gain_vector: bfloat16 [8192], P('tp'), may hold values from 0.25 to 1.75
- gate_matrix: bfloat16 [8192, 16384], P('tp', 'wide'), may hold values from -0.0625 to 0.0625
- up_matrix: bfloat16 [8192, 16384], P('tp', 'wide'), may hold values from -0.0625 to 0.0625
- down_matrix: bfloat16 [16384, 8192], P('wide', 'tp'), may hold values from -0.046875 to 0.046875
- adapter_input_maps: bfloat16 [32, 8192, 32], P(('groups', 'wide'), 'tp'), parts along dimension 0, may hold values from -0.0625 to 0.0625
- adapter_output_maps: bfloat16 [32, 32, 16384], P('groups', 'tp', 'wide'), parts along dimension 0, may hold values from -1.5 to 1.5
- down_adapter_input: bfloat16 [32, 16, 16384], P('groups', None, ('wide', 'tp')), parts along dimension 0, may hold values from -0.046875 to 0.046875
- down_adapter_output: bfloat16 [32, 16, 8192], P(('groups', 'wide'), None, 'tp'), parts along dimension 0, may hold values from -1.5 to 1.5
- request_adapter: int32 [256], P('groups'), parts along dimension 0, may hold values from 0 to 15
- adapter_storage_slot: int32 [32], P('groups'), parts along dimension 0, may hold values from 0 to 15, each once
Outputs:
- layer_out: bfloat16 [256, 8192], P(('groups', 'wide'), 'tp'), parts along dimension 0
The draws below stay inside these ranges and needn't reach their ends.
There are 2 independent parts, one for each index of `groups`. The reference program is written for one: setup_inputs(seed, part) draws one part's arguments, and reference() takes and returns one part's arrays. A program takes and returns all parts, laid end to end along the dimension named above; an argument that names none is the same for every part. Nothing has to cross between parts.
Inputs may be any that keep to these rules, and one draw needn't show every extreme that they name: `adapter_storage_slot`: a permutation of the slots. The 128 lengths of each group sum to 16384, and some request of each group fills its whole cache.
All inputs are finite; a program needn't handle non-finite values.
Results may differ from the reference program's by a relative error of at most 0.014.
Values may be sent and summed in bfloat16 or wider, within the bound.
A program may use at most 192 MiB of HBM per device.

```python
import math
import jax
import jax.numpy as jnp
import numpy as np
from jax import lax

MODEL_WIDTH = 8192
HEADS = 64
KVH = 8
HD = 128
FEEDFWD_UNITS = 16384
ADAPTER_RANK = 16
CTX = 256
REQUEST_TOTAL = 128
ADAPTER_TOTAL = 16


def draw_queries(key, part):
    key = jax.random.fold_in(key, 11)
    first_key = jax.random.fold_in(key, 0)
    group_size = HEADS // KVH
    values = jnp.clip(jax.random.normal(first_key, (REQUEST_TOTAL, KVH, group_size, HD), jnp.float32), -6.0, 6.0)
    return values.reshape(REQUEST_TOTAL, HEADS * HD).astype(jnp.bfloat16)


def draw_cached_key_rows(key, part):
    key = jax.random.fold_in(key, 23)
    first_key = jax.random.fold_in(key, 0)
    values = jnp.clip(jax.random.normal(first_key, (REQUEST_TOTAL, KVH, CTX, HD), jnp.float32), -6.0, 6.0)
    return values.astype(jnp.bfloat16)


def feature_scales(low_log, high_log):
    position = jnp.arange(MODEL_WIDTH, dtype=jnp.float32) / jnp.float32(max(MODEL_WIDTH - 1, 1))
    return jnp.exp(low_log + (high_log - low_log) * position)


def draw_residual(key, part):
    key = jax.random.fold_in(key, 37)
    first_key = jax.random.fold_in(key, 0)
    noise = jnp.clip(jax.random.normal(first_key, (REQUEST_TOTAL, MODEL_WIDTH), jnp.float32), -6.0, 6.0)
    values = noise * feature_scales(-0.55, 0.55)[None, :]
    return values.astype(jnp.bfloat16)


def with_ends(array, key, low, largest):
    dims = array.shape
    place = [jax.random.randint(jax.random.fold_in(key, axis), (), 0, dims[axis]) for axis in range(len(dims))]
    array = array.at[tuple(place)].set(low)
    longest = dims.index(max(dims))
    place[longest] = (place[longest] + 1) % dims[longest]
    return array.at[tuple(place)].set(largest)


def levels(own_key, dims, pieces, smallest, largest):
    loudness = 1.0
    for axis_at, shards_of in pieces:
        draws = jax.random.uniform(jax.random.fold_in(jax.random.fold_in(own_key, 6), axis_at), (shards_of,), jnp.float32, smallest / len(pieces), largest / len(pieces))
        loudness = loudness * jnp.repeat(jnp.exp(draws), dims[axis_at] // shards_of).reshape((-1,) + (1,) * (len(dims) - 1 - axis_at))
    return loudness


def cumulative_ranks(count, skew):
    weights = [(1 << 20) // math.isqrt(standing ** skew) + 1 for standing in range(1, count + 1)]
    deviation = 1 + sum(weights) // (1 << 30)
    return np.cumsum(np.array([max(1, weight // deviation) for weight in weights]))


def skewed_ids(own_key, dims, amount, skew):
    table = cumulative_ranks(amount, skew)
    pick = jax.random.randint(jax.random.fold_in(own_key, 1), dims, 0, int(table[amount - 1]))
    rank = jnp.searchsorted(jnp.asarray(table, jnp.int32), pick, side="right")
    return jax.random.permutation(jax.random.fold_in(own_key, 2), amount)[rank].astype(jnp.int32)


def length_profile(number_of, total, most, skew):
    loads = [(1 << 20) // math.isqrt(standing ** skew) + 1 for standing in range(2, number_of + 1)]
    rest, holding = total - most - (number_of - 1), [1] * (number_of - 1)
    while rest > 0:
        movable = [i for i in range(number_of - 1) if holding[i] < most]
        mass, budget = sum([loads[i] for i in movable]), rest
        for i in movable:
            extra = min(most - holding[i], max(1, budget * loads[i] // mass), rest)
            holding[i] = holding[i] + extra
            rest = rest - extra
    return np.array([most] + holding)


def ragged(rng, count, total, limit, slope):
    if count == 2:
        one = jax.random.randint(rng, (), max(1, total - limit), min(limit, total - 1) + 1)
        return jnp.stack([one, total - one])
    sizes = jnp.asarray(length_profile(count, total, limit, slope), jnp.int32)
    couples = (count - 1) // 2
    source_of, receiver = sizes[1:1 + 2 * couples:2], sizes[2:2 + 2 * couples:2]
    slack = jnp.minimum(source_of - 1, limit - receiver)
    moved = jax.random.randint(jax.random.fold_in(rng, 1), (couples,), 0, 1 << 20) % (slack + 1)
    sizes = sizes.at[1:1 + 2 * couples:2].set(source_of - moved).at[2:2 + 2 * couples:2].set(receiver + moved)
    return sizes[jax.random.permutation(jax.random.fold_in(rng, 2), count)]


def gaussian(stream_key, shape, deviation, most, cuts=(), kind=jnp.bfloat16):
    array = deviation * jax.random.normal(stream_key, shape, jnp.float32)
    if cuts:
        array = array * levels(stream_key, shape, cuts, -0.22, 0.18)
    return jnp.clip(array, -most, most).astype(kind)


def setup_inputs(seed: int = 0, part: int = 0) -> dict:
    key_of = jax.random.split(jax.random.key(seed), 18)
    part_splits = jax.random.split(jax.random.fold_in(key_of[17], part), 18)
    queries = draw_queries(jax.random.fold_in(jax.random.fold_in(key_of[17], part), 71), part)
    cached_key_rows = draw_cached_key_rows(jax.random.fold_in(jax.random.fold_in(key_of[17], part), 71), part)
    cached_value_rows = gaussian(part_splits[2], (REQUEST_TOTAL, KVH, CTX, HD), 1.0, 6.0, ((0, 4), (1, 4)))
    fresh_token_key = gaussian(part_splits[3], (REQUEST_TOTAL, KVH * HD), 1.0, 6.0, ((0, 4), (1, 4)))
    fresh_token_value = gaussian(part_splits[4], (REQUEST_TOTAL, KVH * HD), 1.0, 6.0, ((0, 4), (1, 4)))
    lengths = ragged(part_splits[5], REQUEST_TOTAL, REQUEST_TOTAL * CTX // 2, CTX, 2).astype(jnp.int32)
    residual = draw_residual(jax.random.fold_in(jax.random.fold_in(key_of[17], part), 71), part)
    norm_gain_vector = jnp.clip(1.0 + 0.15 * jax.random.normal(key_of[7], (MODEL_WIDTH,), jnp.float32), 0.25, 1.75).astype(jnp.bfloat16)
    gate_matrix = gaussian(key_of[8], (MODEL_WIDTH, FEEDFWD_UNITS), MODEL_WIDTH ** -0.5, 0.0625, ((0, 4), (1, 4)))
    up_matrix = gaussian(key_of[9], (MODEL_WIDTH, FEEDFWD_UNITS), MODEL_WIDTH ** -0.5, 0.0625, ((0, 4), (1, 4)))
    down_matrix = gaussian(key_of[10], (FEEDFWD_UNITS, MODEL_WIDTH), FEEDFWD_UNITS ** -0.5, 0.046875, ((0, 4), (1, 4)))
    adapter_input_maps = gaussian(part_splits[11], (ADAPTER_TOTAL, MODEL_WIDTH, 2 * ADAPTER_RANK), MODEL_WIDTH ** -0.5, 0.0625, ((0, 4), (1, 4)))
    adapter_output_maps = gaussian(part_splits[12], (ADAPTER_TOTAL, 2 * ADAPTER_RANK, FEEDFWD_UNITS), ADAPTER_RANK ** -0.5, 1.5, ((1, 4), (2, 4)))
    down_adapter_input = gaussian(part_splits[13], (ADAPTER_TOTAL, ADAPTER_RANK, FEEDFWD_UNITS), FEEDFWD_UNITS ** -0.5, 0.046875, ((2, 16),))
    down_adapter_output = gaussian(part_splits[14], (ADAPTER_TOTAL, ADAPTER_RANK, MODEL_WIDTH), ADAPTER_RANK ** -0.5, 1.5, ((0, 4), (2, 4)))
    request_adapter = with_ends(skewed_ids(part_splits[15], (REQUEST_TOTAL,), ADAPTER_TOTAL, 2), jax.random.fold_in(part_splits[15], 3), 0, ADAPTER_TOTAL - 1).astype(jnp.int32)
    adapter_storage_slot = jax.random.permutation(part_splits[16], ADAPTER_TOTAL).astype(jnp.int32)
    return dict(queries=queries, cached_key_rows=cached_key_rows, cached_value_rows=cached_value_rows, fresh_token_key=fresh_token_key, fresh_token_value=fresh_token_value, lengths=lengths, residual=residual, norm_gain_vector=norm_gain_vector, gate_matrix=gate_matrix, up_matrix=up_matrix, down_matrix=down_matrix, adapter_input_maps=adapter_input_maps, adapter_output_maps=adapter_output_maps, down_adapter_input=down_adapter_input, down_adapter_output=down_adapter_output, request_adapter=request_adapter, adapter_storage_slot=adapter_storage_slot)


def reference(queries, cached_key_rows, cached_value_rows, fresh_token_key, fresh_token_value, lengths, residual, norm_gain_vector, gate_matrix, up_matrix, down_matrix, adapter_input_maps, adapter_output_maps, down_adapter_input, down_adapter_output, request_adapter, adapter_storage_slot):
    group_size = HEADS // KVH
    score_scale = 1.0 / math.sqrt(HD)
    query_heads = queries.astype(jnp.float32).reshape(REQUEST_TOTAL, KVH, group_size, HD)
    scores = jnp.einsum('rkgd,rkld->rkgl', query_heads, cached_key_rows.astype(jnp.float32)) * score_scale
    own_score = jnp.einsum('rkgd,rkd->rkg', query_heads, fresh_token_key.astype(jnp.float32).reshape(REQUEST_TOTAL, KVH, HD)) * score_scale
    visible = lax.broadcasted_iota(jnp.int32, (REQUEST_TOTAL, CTX), 1) < lengths[:, None]
    scores = jnp.where(visible[:, None, None, :], scores, jnp.float32(-1e+30))
    row_peak = jnp.maximum(lax.optimization_barrier(jnp.max(scores, axis=-1)), own_score)
    weights = jnp.exp(scores - row_peak[..., None])
    own_weight = jnp.exp(own_score - row_peak)
    denominator = lax.optimization_barrier(jnp.sum(weights, axis=-1)) + own_weight
    weights_low = lax.optimization_barrier(weights.astype(jnp.bfloat16)).astype(jnp.float32)
    fresh_value = fresh_token_value.astype(jnp.float32).reshape(REQUEST_TOTAL, KVH, HD)
    mixed = jnp.einsum('rkgl,rkld->rkgd', weights_low, cached_value_rows.astype(jnp.float32))
    mixed = mixed + own_weight[..., None] * fresh_value[:, :, None, :]
    attn = (mixed / denominator[..., None]).reshape(REQUEST_TOTAL, MODEL_WIDTH).astype(jnp.bfloat16)
    stream = (residual.astype(jnp.float32) + attn.astype(jnp.float32)).astype(jnp.bfloat16)
    as_float = stream.astype(jnp.float32)
    mean_square = lax.optimization_barrier(jnp.mean(as_float * as_float, axis=-1, keepdims=True))
    normed = (as_float * lax.rsqrt(mean_square + 1e-05) * norm_gain_vector.astype(jnp.float32)).astype(jnp.bfloat16)
    adapter_ids = lax.broadcasted_iota(jnp.int32, (REQUEST_TOTAL, ADAPTER_TOTAL), 1)
    adapter_hits = request_adapter[:, None] == adapter_ids
    slot_of_row = lax.optimization_barrier(jnp.sum(jnp.where(adapter_hits, adapter_storage_slot[None, :], 0), axis=1)).astype(jnp.int32)
    slot_hits = slot_of_row[:, None] == adapter_ids
    inner_lookup = jnp.transpose(adapter_input_maps, (1, 0, 2)).reshape(MODEL_WIDTH, ADAPTER_TOTAL * 2 * ADAPTER_RANK)
    inner_all = jnp.dot(normed, inner_lookup, preferred_element_type=jnp.float32).reshape(REQUEST_TOTAL, ADAPTER_TOTAL, 2 * ADAPTER_RANK)
    inner = lax.optimization_barrier(jnp.sum(jnp.where(slot_hits[:, :, None], inner_all, jnp.float32(0.0)), axis=1)).astype(jnp.bfloat16)
    positioned = jnp.where(slot_hits[:, :, None], inner[:, None, :], jnp.bfloat16(0.0)).astype(jnp.bfloat16)
    gate_adapter_term = jnp.dot(positioned[:, :, :ADAPTER_RANK].reshape(REQUEST_TOTAL, ADAPTER_TOTAL * ADAPTER_RANK), adapter_output_maps[:, :ADAPTER_RANK, :].reshape(ADAPTER_TOTAL * ADAPTER_RANK, FEEDFWD_UNITS), preferred_element_type=jnp.float32)
    up_adapter_term = jnp.dot(positioned[:, :, ADAPTER_RANK:].reshape(REQUEST_TOTAL, ADAPTER_TOTAL * ADAPTER_RANK), adapter_output_maps[:, ADAPTER_RANK:, :].reshape(ADAPTER_TOTAL * ADAPTER_RANK, FEEDFWD_UNITS), preferred_element_type=jnp.float32)
    gate = jnp.dot(normed, gate_matrix, preferred_element_type=jnp.float32) + gate_adapter_term
    up_value = jnp.dot(normed, up_matrix, preferred_element_type=jnp.float32) + up_adapter_term
    hidden_state = (jax.nn.silu(gate) * up_value).astype(jnp.bfloat16)
    down_gathered = jnp.einsum('tv,ywv->tyw', hidden_state.astype(jnp.float32), down_adapter_input.astype(jnp.float32))
    down_low = lax.optimization_barrier(jnp.sum(jnp.where(slot_hits[:, :, None], down_gathered, jnp.float32(0.0)), axis=1)).astype(jnp.bfloat16)
    down_positioned = jnp.where(slot_hits[:, :, None], down_low[:, None, :], jnp.bfloat16(0.0)).astype(jnp.bfloat16)
    adapter_change = jnp.dot(down_positioned.reshape(REQUEST_TOTAL, ADAPTER_TOTAL * ADAPTER_RANK), down_adapter_output.reshape(ADAPTER_TOTAL * ADAPTER_RANK, MODEL_WIDTH), preferred_element_type=jnp.float32)
    projected = jnp.dot(hidden_state, down_matrix, preferred_element_type=jnp.float32) + adapter_change
    return (stream.astype(jnp.float32) + projected).astype(jnp.bfloat16)
```

```python
import math

import jax
import jax.numpy as jnp
from jax import lax
from jax.experimental import pallas as pl
from jax.experimental.pallas import tpu as pltpu
from jax.sharding import PartitionSpec as P

MESH = pl.DeviceIdType.MESH
NT = (((1,), (1,)), ((), ()))
TN = (((0,), (0,)), ((), ()))


def feed_forward_kernel(
    slot_ref, stream_ref, gain_ref, ain_hbm, omap_hbm, dai_hbm, dout_hbm, gate_hbm, up_hbm, down_hbm,
    out_ref,
    raw, x, ain, omap, dai, dout, w, dw,
    ex_send, ex_recv, pf, s1_send, s1_recv, fwd, own, s2_send, s2_recv,
    hid, dinner, dx_send, dx_recv, acc, o_send, o_recv,
    small_sem, w_sem, dw_sem,
    raw_ss, raw_rs, ex_ss, ex_rs, s1_ss, s1_rs, s2_ss, s2_rs, h_ss, h_rs, dx_ss, dx_rs, o_ss, o_rs,
):
    f32, bf16 = jnp.float32, jnp.bfloat16
    rows, width = stream_ref.shape
    total = 4 * rows
    sub = w.shape[2] // 2
    me_w, z = lax.axis_index("wide"), lax.axis_index("tp")
    me = me_w * 4 + z
    z1 = z + 1 - 2 * lax.rem(z, 2)
    z2 = lax.rem(z + 2, 4)
    z3 = 3 - z
    quarters = (z3, z2, z1, z)

    def column(q, b):
        return pl.multiple_of((q * 4 + b) * sub, sub)

    def w_copy(slot, b, i, start):
        half, parts = slot * 4 + i, []
        for j, src in enumerate((gate_hbm, up_hbm)):
            parts.append(pltpu.make_async_copy(
                src.at[:, pl.ds(column(quarters[i], b), sub)],
                w.at[half, :, pl.ds(j * sub, sub)], w_sem.at[half, j]))
        for part in parts:
            part.start() if start else part.wait()

    def dw_copy(k):
        return pltpu.make_async_copy(
            down_hbm.at[pl.ds(pl.multiple_of(k * sub, sub), sub), :], dw.at[k], dw_sem.at[k])

    def small_copy(j):
        src, dst = ((ain_hbm, ain), (omap_hbm, omap), (dai_hbm, dai), (dout_hbm, dout))[j]
        return pltpu.make_async_copy(src, dst, small_sem.at[j])

    def remote(src, dst, ss, rs, dev_w, dev_t):
        return pltpu.make_async_remote_copy(
            src_ref=src, dst_ref=dst, send_sem=ss, recv_sem=rs,
            device_id={"wide": dev_w, "tp": dev_t}, device_id_type=MESH)

    barrier = pltpu.get_barrier_semaphore()

    def greet(e, carry):
        peer = lax.rem(me + e, 16)
        pl.semaphore_signal(barrier, inc=1, device_id={"wide": peer // 4, "tp": lax.rem(peer, 4)},
                            device_id_type=MESH)
        return carry

    lax.fori_loop(1, 16, greet, 0)
    small_copy(0).start()
    for slot in range(2):
        for i in range(4):
            w_copy(slot, slot, i, True)
        if slot == 0:
            small_copy(1).start()
    small_copy(2).start()
    small_copy(3).start()
    raw[me_w] = stream_ref[...]
    pl.semaphore_wait(barrier, 15)

    def raw_copy(owner, d, dev):
        return remote(raw.at[owner], raw.at[owner], raw_ss.at[d - 1], raw_rs.at[owner], dev, z)

    for d in (1, 2, 3):
        raw_copy(me_w, d, lax.rem(me_w + d, 4)).start()

    def dw_start(k, carry):
        dw_copy(k).start()
        return carry

    lax.fori_loop(0, 16, dw_start, 0)
    for d in (1, 2, 3):
        peer = lax.rem(me_w + d, 4)
        raw_copy(peer, d, peer).wait_recv()
    gain = gain_ref[...].astype(f32)
    squares = []
    for p in range(4):
        part = raw[p].astype(f32)
        squares.append(jnp.sum(part * part, axis=1, keepdims=True))
        x[pl.ds(p * rows, rows), :] = (part * gain).astype(bf16)
    square = jnp.broadcast_to(jnp.concatenate(squares, axis=0), (total, total)).T

    slot_row = slot_ref[...]
    small_copy(0).wait()
    inner = lax.dot_general(ain[...], x[...], NT, preferred_element_type=f32)
    chosen = jnp.zeros((32, total), f32)
    for a in range(4):
        chosen = chosen + jnp.where(slot_row == me_w * 4 + a, inner[a * 32:(a + 1) * 32], 0.0)
    for t in range(4):
        ex_send[t, 0:8, :] = chosen[t * 8:(t + 1) * 8]
        ex_send[t, 8:16, :] = square[0:8]

    def ex_start(e, carry):
        peer = lax.rem(me + e, 16)
        pt = lax.rem(peer, 4)
        remote(ex_send.at[pt], ex_recv.at[me], ex_ss.at[e], ex_rs.at[me], peer // 4, pt).start()
        return carry

    lax.fori_loop(1, 16, ex_start, 0)
    ex_recv[me] = ex_send[z]

    def fill(b):
        slot = lax.rem(b, 2)
        for i in range(4):
            w_copy(slot, b, i, False)
            pf[i] = jnp.dot(x[...], w[slot * 4 + i], preferred_element_type=f32)

        @pl.when(b < 2)
        def _():
            for i in range(4):
                w_copy(slot, b + 2, i, True)

    fill(jnp.int32(0))

    def ex_wait(e, carry):
        peer = lax.rem(me + e, 16)
        desc = remote(ex_send.at[z], ex_recv.at[peer], ex_ss.at[e], ex_rs.at[peer], peer // 4, lax.rem(peer, 4))
        desc.wait_recv()
        desc.wait_send()
        return carry

    lax.fori_loop(1, 16, ex_wait, 0)
    low = ex_recv[0, 0:8, :]
    for e in range(1, 16):
        low = low + ex_recv[e, 0:8, :]
    square = ex_recv[me_w * 4, 8:16, :]
    for t in range(1, 4):
        square = square + ex_recv[me_w * 4 + t, 8:16, :]
    scale_row = lax.rsqrt(square / f32(width * 4) + 1e-05)
    scale = jnp.broadcast_to(scale_row[0:1], (total, total)).T
    scale = jnp.concatenate([scale] * (sub // total), axis=1)
    placed = jnp.concatenate([jnp.where(slot_row == a, low, 0.0) for a in range(16)], axis=0).T.astype(bf16)
    is_gate = z < 2
    small_copy(1).wait()

    def s1_copy(j, b):
        return remote(s1_send.at[j, b], s1_recv.at[j, b], s1_ss.at[j, b], s1_rs.at[j, b], me_w, z1)

    def s2_copy(b):
        return remote(s2_send.at[b], s2_recv.at[b], s2_ss.at[b], s2_rs.at[b], me_w, z2)

    def pass_on(b):
        s1_copy(0, b).wait_recv()
        s2_send[b] = (fwd[b] + s1_recv[0, b].astype(f32)).astype(bf16)
        s2_copy(b).start()

    def spread(b, carry):
        for i in range(4):
            term = jnp.dot(placed, omap[:, pl.ds(column(quarters[i], b), sub)], preferred_element_type=f32)
            value = pf[i] + jnp.concatenate(
                [jnp.where(is_gate, term, 0.0), jnp.where(is_gate, 0.0, term)], axis=1)
            if i == 1:
                fwd[b] = value
            elif i == 3:
                own[b] = value
            else:
                s1_send[i // 2, b] = value.astype(bf16)
                s1_copy(i // 2, b).start()

        @pl.when(b < 3)
        def _():
            fill(b + 1)

        @pl.when(b > 0)
        def _():
            pass_on(b - 1)

        return carry

    lax.fori_loop(0, 4, spread, 0)
    pass_on(jnp.int32(3))

    def h_copy(q, b, d, dev):
        return remote(hid.at[q, b], hid.at[q, b], h_ss.at[d - 1, b], h_rs.at[q, b], me_w, dev)

    def add_product(q, b):
        k = q * 4 + b
        dw_copy(k).wait()
        acc[...] += jnp.dot(hid[q, b], dw[k], preferred_element_type=f32)

    def add_others(b):
        for d in (1, 2, 3):
            q = quarters[3 - d]
            h_copy(q, b, d, q).wait_recv()
            add_product(q, b)

    acc[...] = jnp.zeros_like(acc)
    dinner[...] = jnp.zeros_like(dinner)
    small_copy(2).wait()

    def finish(b, carry):
        s1_copy(1, b).wait_recv()
        s2_copy(b).wait_recv()
        value = own[b] + s1_recv[1, b].astype(f32) + s2_recv[b].astype(f32)
        gate = value[:, :sub] * scale
        up = value[:, sub:] * scale
        hid[z, b] = (gate / (1.0 + jnp.exp(-gate)) * up).astype(bf16)
        for d in (3, 2, 1):
            h_copy(z, b, d, quarters[3 - d]).start()
        dinner[...] += lax.dot_general(
            dai[:, pl.ds(pl.multiple_of(b * sub, sub), sub)], hid[z, b], NT, preferred_element_type=f32)
        add_product(z, b)

        @pl.when(b > 0)
        def _():
            add_others(b - 1)

        return carry

    lax.fori_loop(0, 4, finish, 0)

    down_low = jnp.zeros((16, total), f32)
    for a in range(16):
        down_low = down_low + jnp.where(slot_row == a, dinner[a * 16:(a + 1) * 16, :], 0.0)
    dx_send[...] = down_low
    dx_recv[me] = down_low

    def dx_copy(owner, e, peer):
        return remote(dx_send, dx_recv.at[owner], dx_ss.at[e], dx_rs.at[owner], peer // 4, lax.rem(peer, 4))

    def dx_start(e, carry):
        dx_copy(me, e, lax.rem(me + e, 16)).start()
        return carry

    lax.fori_loop(1, 16, dx_start, 0)
    add_others(jnp.int32(3))

    def dx_wait(e, carry):
        peer = lax.rem(me + e, 16)
        dx_copy(peer, e, peer).wait_recv()
        dx_copy(peer, e, peer).wait_send()
        return carry

    lax.fori_loop(1, 16, dx_wait, 0)
    down_low = dx_recv[0]
    for e in range(1, 16):
        down_low = down_low + dx_recv[e]
    placed_down = jnp.concatenate(
        [jnp.where(slot_row == me_w * 4 + a, down_low, 0.0) for a in range(4)], axis=0).astype(bf16)
    small_copy(3).wait()
    acc[...] += lax.dot_general(placed_down, dout[...], TN, preferred_element_type=f32)

    def o_copy(d, dev):
        return remote(o_send.at[d - 1], o_recv.at[d - 1], o_ss.at[d - 1], o_rs.at[d - 1], dev, z)

    for d in (2, 3, 1):
        peer = lax.rem(me_w + d, 4)
        o_send[d - 1] = acc[pl.ds(pl.multiple_of(peer * rows, rows), rows), :].astype(bf16)
        o_copy(d, peer).start()
    result = stream_ref[...].astype(f32) + acc[pl.ds(pl.multiple_of(me_w * rows, rows), rows), :]
    for d in (1, 2, 3):
        o_copy(d, lax.rem(me_w + d, 4)).wait_recv()
        result = result + o_recv[d - 1].astype(f32)
    out_ref[...] = result.astype(bf16)

    for d in (1, 2, 3):
        peer = lax.rem(me_w + d, 4)
        raw_copy(me_w, d, peer).wait_send()
        o_copy(d, peer).wait_send()

    def drain(b, carry):
        s1_copy(0, b).wait_send()
        s1_copy(1, b).wait_send()
        s2_copy(b).wait_send()
        for d in (1, 2, 3):
            h_copy(z, b, d, quarters[3 - d]).wait_send()
        return carry

    lax.fori_loop(0, 4, drain, 0)


def feed_forward(stream, norm_gain, gate, up, down, ain, omaps, dai, dout, slot_of_row):
    rows, width = stream.shape
    total = 4 * rows
    hidden = gate.shape[1]
    sub = hidden // 16
    owned, _, rank2 = ain.shape
    f32, bf16 = jnp.float32, jnp.bfloat16
    ain_t = jnp.transpose(ain, (0, 2, 1)).reshape(owned * rank2, width)
    omap = omaps.reshape(omaps.shape[0] * omaps.shape[1], hidden)
    dai2 = dai.reshape(dai.shape[0] * dai.shape[1], dai.shape[2])
    dout2 = dout.reshape(dout.shape[0] * dout.shape[1], width)
    dma = pltpu.SemaphoreType.DMA
    vmem = pl.BlockSpec(memory_space=pltpu.VMEM)
    hbm = pl.BlockSpec(memory_space=pl.ANY)
    return pl.pallas_call(
        feed_forward_kernel,
        out_shape=jax.ShapeDtypeStruct((rows, width), bf16),
        in_specs=[vmem] * 3 + [hbm] * 7,
        out_specs=vmem,
        scratch_shapes=[
            pltpu.VMEM((4, rows, width), bf16),
            pltpu.VMEM((total, width), bf16),
            pltpu.VMEM(ain_t.shape, bf16),
            pltpu.VMEM(omap.shape, bf16),
            pltpu.VMEM(dai2.shape, bf16),
            pltpu.VMEM(dout2.shape, bf16),
            pltpu.VMEM((8, width, 2 * sub), bf16),
            pltpu.VMEM((16, sub, width), bf16),
            pltpu.VMEM((4, 16, total), f32),
            pltpu.VMEM((16, 16, total), f32),
            pltpu.VMEM((4, total, 2 * sub), f32),
            pltpu.VMEM((2, 4, total, 2 * sub), bf16),
            pltpu.VMEM((2, 4, total, 2 * sub), bf16),
            pltpu.VMEM((4, total, 2 * sub), f32),
            pltpu.VMEM((4, total, 2 * sub), f32),
            pltpu.VMEM((4, total, 2 * sub), bf16),
            pltpu.VMEM((4, total, 2 * sub), bf16),
            pltpu.VMEM((4, 4, total, sub), bf16),
            pltpu.VMEM((dai2.shape[0], total), f32),
            pltpu.VMEM((16, total), f32),
            pltpu.VMEM((16, 16, total), f32),
            pltpu.VMEM((total, width), f32),
            pltpu.VMEM((3, rows, width), bf16),
            pltpu.VMEM((3, rows, width), bf16),
            dma((4,)), dma((8, 2)), dma((16,)),
            dma((3,)), dma((4,)), dma((16,)), dma((16,)),
            dma((2, 4)), dma((2, 4)), dma((4,)), dma((4,)),
            dma((3, 4)), dma((4, 4)), dma((16,)), dma((16,)), dma((3,)), dma((3,)),
        ],
        compiler_params=pltpu.CompilerParams(
            collective_id=0, has_side_effects=True, vmem_limit_bytes=58 * 2**20),
        cost_estimate=pl.CostEstimate(
            flops=6 * total * width * hidden, bytes_accessed=6 * width * hidden, transcendentals=0),
    )(slot_of_row.reshape(1, total), stream, norm_gain.reshape(1, width), ain_t, omap, dai2, dout2,
      gate, up, down)


def per_device(
    queries,
    cached_key_rows,
    cached_value_rows,
    fresh_token_key,
    fresh_token_value,
    lengths,
    residual,
    norm_gain_vector,
    gate_matrix,
    up_matrix,
    down_matrix,
    adapter_input_maps,
    adapter_output_maps,
    down_adapter_input,
    down_adapter_output,
    request_adapter,
    adapter_storage_slot,
):
    rows_here = queries.shape[0]
    kv_here = cached_key_rows.shape[1]
    context = cached_key_rows.shape[2]
    head_size = cached_key_rows.shape[3]
    group_size = queries.shape[1] // (kv_here * head_size)
    score_scale = 1.0 / math.sqrt(head_size)
    query_heads = queries.reshape(rows_here, kv_here, group_size, head_size)
    scores = (
        jnp.einsum(
            "rkgd,rkld->rkgl", query_heads, cached_key_rows, preferred_element_type=jnp.float32
        )
        * score_scale
    )
    own_score = (
        jnp.einsum(
            "rkgd,rkd->rkg",
            query_heads,
            fresh_token_key.reshape(rows_here, kv_here, head_size),
            preferred_element_type=jnp.float32,
        )
        * score_scale
    )
    visible = lax.broadcasted_iota(jnp.int32, (rows_here, context), 1) < lengths[:, None]
    scores = jnp.where(visible[:, None, None, :], scores, jnp.float32(-1e30))
    row_peak = jnp.maximum(jnp.max(scores, axis=-1), own_score)
    weights = jnp.exp(scores - row_peak[..., None])
    own_weight = jnp.exp(own_score - row_peak)
    denominator = jnp.sum(weights, axis=-1) + own_weight
    fresh_value = fresh_token_value.reshape(rows_here, kv_here, head_size).astype(jnp.float32)
    mixed = jnp.einsum(
        "rkgl,rkld->rkgd",
        weights.astype(jnp.bfloat16),
        cached_value_rows,
        preferred_element_type=jnp.float32,
    )
    mixed = mixed + own_weight[..., None] * fresh_value[:, :, None, :]
    attn = (mixed / denominator[..., None]).reshape(rows_here, -1).astype(jnp.bfloat16)
    stream = (residual.astype(jnp.float32) + attn.astype(jnp.float32)).astype(jnp.bfloat16)
    if lax.axis_size("tp") == 4 and lax.axis_size("wide") == 4 and rows_here == 32:
        ids = lax.broadcasted_iota(
            jnp.int32, (request_adapter.shape[0], adapter_storage_slot.shape[0]), 1
        )
        slots = jnp.sum(
            jnp.where(request_adapter[:, None] == ids, adapter_storage_slot[None, :], 0), axis=1
        )
        return feed_forward(
            stream,
            norm_gain_vector,
            gate_matrix,
            up_matrix,
            down_matrix,
            adapter_input_maps,
            adapter_output_maps,
            down_adapter_input,
            down_adapter_output,
            slots,
        )
    tp_count = lax.axis_size("tp")
    my_tp = lax.axis_index("tp")
    my_wide = lax.axis_index("wide")
    width_portion = residual.shape[1]
    as_float = stream.astype(jnp.float32)
    square_sum = lax.psum(jnp.sum(as_float * as_float, axis=1, keepdims=True), "tp")
    mean_square = square_sum / jnp.float32(width_portion * tp_count)
    normed = (
        as_float * lax.rsqrt(mean_square + 1e-05) * norm_gain_vector.astype(jnp.float32)[None, :]
    ).astype(jnp.bfloat16)
    owned_number = adapter_input_maps.shape[0]
    adapter_number = adapter_output_maps.shape[0]
    rank_portion = adapter_output_maps.shape[1]
    adapter_rank_size = down_adapter_input.shape[1]
    hidden_portion = gate_matrix.shape[1]
    subset_width = down_adapter_input.shape[2]
    every_request_row = request_adapter.shape[0]
    adapter_ids = lax.broadcasted_iota(jnp.int32, (every_request_row, adapter_number), 1)
    adapter_hits = request_adapter[:, None] == adapter_ids
    slot_of_row = jnp.sum(jnp.where(adapter_hits, adapter_storage_slot[None, :], 0), axis=1)
    slot_hits = slot_of_row[:, None] == adapter_ids
    owned_ids = my_wide * owned_number + lax.broadcasted_iota(
        jnp.int32, (every_request_row, owned_number), 1
    )
    local_hits = slot_of_row[:, None] == owned_ids
    inner_lookup = jnp.transpose(adapter_input_maps, (1, 0, 2)).reshape(
        width_portion, owned_number * 2 * adapter_rank_size
    )
    block_rows = lax.all_gather(normed, "wide", axis=0, tiled=True)
    request_number = block_rows.shape[0]
    gate_part = jnp.dot(block_rows, gate_matrix, preferred_element_type=jnp.float32)
    up_part = jnp.dot(block_rows, up_matrix, preferred_element_type=jnp.float32)
    inner_all = jnp.dot(block_rows, inner_lookup, preferred_element_type=jnp.float32).reshape(
        request_number, owned_number, 2 * adapter_rank_size
    )
    inner_part = jnp.sum(jnp.where(local_hits[:, :, None], inner_all, jnp.float32(0.0)), axis=1)
    joined = jnp.concatenate([gate_part, up_part, inner_part], axis=1)
    inner_sum = lax.psum(joined[:, 2 * hidden_portion :], ("wide", "tp"))
    inner_low = inner_sum.astype(jnp.bfloat16)
    positioned = jnp.where(slot_hits[:, :, None], inner_low[:, None, :], jnp.bfloat16(0.0))
    rank_start = my_tp * rank_portion
    placed_slice = lax.dynamic_slice_in_dim(positioned, rank_start, rank_portion, 2)
    rank_position = rank_start + lax.broadcasted_iota(jnp.int32, (rank_portion,), 0)
    gate_select_mask = rank_position < adapter_rank_size
    gate_input = jnp.where(
        gate_select_mask[None, None, :], placed_slice, jnp.bfloat16(0.0)
    ).reshape(every_request_row, adapter_number * rank_portion)
    up_input = jnp.where(gate_select_mask[None, None, :], jnp.bfloat16(0.0), placed_slice).reshape(
        every_request_row, adapter_number * rank_portion
    )
    output_lookup = adapter_output_maps.reshape(adapter_number * rank_portion, hidden_portion)
    gate_pre = joined[:, :hidden_portion] + jnp.dot(
        gate_input, output_lookup, preferred_element_type=jnp.float32
    )
    up_pre = joined[:, hidden_portion : 2 * hidden_portion] + jnp.dot(
        up_input, output_lookup, preferred_element_type=jnp.float32
    )
    gate_total, up_total = lax.psum((gate_pre, up_pre), "tp")
    hidden_state = (jax.nn.silu(gate_total) * up_total).astype(jnp.bfloat16)
    hidden_subset = lax.dynamic_slice_in_dim(hidden_state, my_tp * subset_width, subset_width, 1)
    down_gathered = lax.dot_general(
        hidden_subset,
        down_adapter_input,
        (((1,), (2,)), ((), ())),
        preferred_element_type=jnp.float32,
    )
    down_part = jnp.sum(jnp.where(slot_hits[:, :, None], down_gathered, jnp.float32(0.0)), axis=1)
    down_low = lax.psum(down_part, ("wide", "tp")).astype(jnp.bfloat16)
    local_positioned = jnp.where(local_hits[:, :, None], down_low[:, None, :], jnp.bfloat16(0.0))
    adapter_change = jnp.dot(
        local_positioned.reshape(every_request_row, owned_number * adapter_rank_size),
        down_adapter_output.reshape(owned_number * adapter_rank_size, width_portion),
        preferred_element_type=jnp.float32,
    )
    product = jnp.dot(hidden_state, down_matrix, preferred_element_type=jnp.float32)
    projected = lax.psum_scatter(product, "wide", scatter_dimension=0, tiled=True)
    projected = projected + lax.psum_scatter(
        adapter_change, "wide", scatter_dimension=0, tiled=True
    )
    return (stream.astype(jnp.float32) + projected).astype(jnp.bfloat16)


def solution(mesh):
    return jax.shard_map(
        per_device,
        mesh=mesh,
        in_specs=(
            P(("groups", "wide"), "tp"),
            P(("groups", "wide"), "tp", None, None),
            P(("groups", "wide"), "tp", None, None),
            P(("groups", "wide"), "tp"),
            P(("groups", "wide"), "tp"),
            P(("groups", "wide")),
            P(("groups", "wide"), "tp"),
            P("tp"),
            P("tp", "wide"),
            P("tp", "wide"),
            P("wide", "tp"),
            P(("groups", "wide"), "tp", None),
            P("groups", "tp", "wide"),
            P("groups", None, ("wide", "tp")),
            P(("groups", "wide"), None, "tp"),
            P("groups"),
            P("groups"),
        ),
        out_specs=P(("groups", "wide"), "tp"),
        check_vma=False,
    )
```

```python
import math

import jax
import jax.numpy as jnp
from jax import lax
from jax.experimental import pallas as pl
from jax.experimental.pallas import tpu as pltpu
from jax.sharding import PartitionSpec as P

MESH = pl.DeviceIdType.MESH
NT = (((1,), (1,)), ((), ()))
TN = (((0,), (0,)), ((), ()))


def feed_forward_kernel(
    storage_ref, request_ref, stream_ref, gain_ref, ain_hbm, omap_hbm, dai_hbm, dout_hbm, gate_hbm, up_hbm, down_hbm,
    out_ref,
    raw, x, ain, omap, dai, dout, w, dw,
    ex_send, ex_recv, pf, s1_send, s1_recv, fwd, own, s2_send, s2_recv,
    hid, dinner, dx_send, dx_recv, acc, o_send, o_recv,
    small_sem, w_sem, dw_sem,
    raw_ss, raw_rs, ex_ss, ex_rs, s1_ss, s1_rs, s2_ss, s2_rs, h_ss, h_rs, dx_ss, dx_rs, o_ss, o_rs,
):
    f32, bf16 = jnp.float32, jnp.bfloat16
    rows, width = stream_ref.shape
    total = 4 * rows
    sub = w.shape[2] // 2
    me_w, z = lax.axis_index("wide"), lax.axis_index("tp")
    me = me_w * 4 + z
    z1 = z + 1 - 2 * lax.rem(z, 2)
    z2 = lax.rem(z + 2, 4)
    z3 = 3 - z
    quarters = (z3, z2, z1, z)

    def column(q, b):
        return pl.multiple_of((q * 4 + b) * sub, sub)

    def w_copy(slot, b, i, start):
        half, parts = slot * 4 + i, []
        for j, src in enumerate((gate_hbm, up_hbm)):
            parts.append(pltpu.make_async_copy(
                src.at[:, pl.ds(column(quarters[i], b), sub)],
                w.at[half, :, pl.ds(j * sub, sub)], w_sem.at[half, j]))
        for part in parts:
            part.start() if start else part.wait()

    def dw_copy(k):
        return pltpu.make_async_copy(
            down_hbm.at[pl.ds(pl.multiple_of(k * sub, sub), sub), :], dw.at[k], dw_sem.at[k])

    def small_copy(j):
        src, dst = ((ain_hbm, ain), (omap_hbm, omap), (dai_hbm, dai), (dout_hbm, dout))[j]
        return pltpu.make_async_copy(src, dst, small_sem.at[j])

    def remote(src, dst, ss, rs, dev_w, dev_t):
        return pltpu.make_async_remote_copy(
            src_ref=src, dst_ref=dst, send_sem=ss, recv_sem=rs,
            device_id={"wide": dev_w, "tp": dev_t}, device_id_type=MESH)

    barrier = pltpu.get_barrier_semaphore()

    def greet(e, carry):
        peer = lax.rem(me + e, 16)
        pl.semaphore_signal(barrier, inc=1, device_id={"wide": peer // 4, "tp": lax.rem(peer, 4)},
                            device_id_type=MESH)
        return carry

    lax.fori_loop(1, 16, greet, 0)
    small_copy(0).start()
    for slot in range(2):
        for i in range(4):
            w_copy(slot, slot, i, True)
        if slot == 0:
            small_copy(1).start()
    small_copy(2).start()
    small_copy(3).start()
    raw[me_w] = stream_ref[...]
    pl.semaphore_wait(barrier, 15)

    def raw_copy(owner, d, dev):
        return remote(raw.at[owner], raw.at[owner], raw_ss.at[d - 1], raw_rs.at[owner], dev, z)

    across = lax.rem(me_w + 2, 4)
    sibling = me_w + 1 - 2 * lax.rem(me_w, 2)
    raw_copy(me_w, 1, across).start()
    raw_copy(me_w, 2, sibling).start()

    def dw_start(k, carry):
        dw_copy(k).start()
        return carry

    lax.fori_loop(0, 16, dw_start, 0)
    raw_copy(across, 1, across).wait_recv()
    raw_copy(across, 3, sibling).start()
    raw_copy(sibling, 2, sibling).wait_recv()
    raw_copy(lax.rem(sibling + 2, 4), 3, sibling).wait_recv()
    gain = gain_ref[...].astype(f32)
    squares = []
    for p in range(4):
        part = raw[p].astype(f32)
        squares.append(jnp.sum(part * part, axis=1, keepdims=True))
        x[pl.ds(p * rows, rows), :] = (part * gain).astype(bf16)
    square = jnp.broadcast_to(jnp.concatenate(squares, axis=0), (total, total)).T

    slot_row = jnp.zeros((1, total), jnp.int32)
    for a in range(16):
        slot_row = slot_row + jnp.where(request_ref[...] == a, storage_ref[a], 0)
    small_copy(0).wait()
    inner = lax.dot_general(ain[...], x[...], NT, preferred_element_type=f32)
    chosen = jnp.zeros((32, total), f32)
    for a in range(4):
        chosen = chosen + jnp.where(slot_row == me_w * 4 + a, inner[a * 32:(a + 1) * 32], 0.0)
    for t in range(4):
        ex_send[t, 0:8, :] = chosen[t * 8:(t + 1) * 8]
        ex_send[t, 8:16, :] = square[0:8]

    def ex_start(e, carry):
        peer = lax.rem(me + e, 16)
        pt = lax.rem(peer, 4)
        remote(ex_send.at[pt], ex_recv.at[me], ex_ss.at[e], ex_rs.at[me], peer // 4, pt).start()
        return carry

    lax.fori_loop(1, 16, ex_start, 0)
    ex_recv[me] = ex_send[z]

    def fill(b):
        slot = lax.rem(b, 2)
        for i in range(4):
            w_copy(slot, b, i, False)
            pf[i] = jnp.dot(x[...], w[slot * 4 + i], preferred_element_type=f32)

        @pl.when(b < 2)
        def _():
            for i in range(4):
                w_copy(slot, b + 2, i, True)

    fill(jnp.int32(0))

    def ex_wait(e, carry):
        peer = lax.rem(me + e, 16)
        desc = remote(ex_send.at[z], ex_recv.at[peer], ex_ss.at[e], ex_rs.at[peer], peer // 4, lax.rem(peer, 4))
        desc.wait_recv()
        desc.wait_send()
        return carry

    lax.fori_loop(1, 16, ex_wait, 0)
    low = ex_recv[0, 0:8, :]
    for e in range(1, 16):
        low = low + ex_recv[e, 0:8, :]
    square = ex_recv[me_w * 4, 8:16, :]
    for t in range(1, 4):
        square = square + ex_recv[me_w * 4 + t, 8:16, :]
    scale_row = lax.rsqrt(square / f32(width * 4) + 1e-05)
    scale = jnp.broadcast_to(scale_row[0:1], (total, total)).T
    scale = jnp.concatenate([scale] * (sub // total), axis=1)
    placed = jnp.concatenate([jnp.where(slot_row == a, low, 0.0) for a in range(16)], axis=0).T.astype(bf16)
    is_gate = z < 2
    small_copy(1).wait()

    def s1_copy(j, b):
        return remote(s1_send.at[j, b], s1_recv.at[j, b], s1_ss.at[j, b], s1_rs.at[j, b], me_w, z1)

    def s2_copy(b):
        return remote(s2_send.at[b], s2_recv.at[b], s2_ss.at[b], s2_rs.at[b], me_w, z2)

    def pass_on(b):
        s1_copy(0, b).wait_recv()
        s2_send[b] = (fwd[b] + s1_recv[0, b].astype(f32)).astype(bf16)
        s2_copy(b).start()

    def h_copy(q, b, d, dev):
        return remote(hid.at[q, b], hid.at[q, b], h_ss.at[d - 1, b], h_rs.at[q, b], me_w, dev)

    def add_product(q, b):
        k = q * 4 + b
        dw_copy(k).wait()
        acc[...] += jnp.dot(hid[q, b], dw[k], preferred_element_type=f32)

    def add_others(b):
        for d in (1, 2, 3):
            q = quarters[3 - d]
            h_copy(q, b, d, q).wait_recv()
            add_product(q, b)

    acc[...] = jnp.zeros_like(acc)
    dinner[...] = jnp.zeros_like(dinner)
    small_copy(2).wait()

    def finish(b, carry):
        s1_copy(1, b).wait_recv()
        s2_copy(b).wait_recv()
        value = own[b] + s1_recv[1, b].astype(f32) + s2_recv[b].astype(f32)
        gate = value[:, :sub] * scale
        up = value[:, sub:] * scale
        hid[z, b] = (gate / (1.0 + jnp.exp(-gate)) * up).astype(bf16)
        for d in (3, 2, 1):
            h_copy(z, b, d, quarters[3 - d]).start()
        dinner[...] += lax.dot_general(
            dai[:, pl.ds(pl.multiple_of(b * sub, sub), sub)], hid[z, b], NT, preferred_element_type=f32)
        add_product(z, b)

        @pl.when(b > 0)
        def _():
            add_others(b - 1)

        return carry

    def spread(b, carry):
        for i in range(4):
            term = jnp.dot(placed, omap[:, pl.ds(column(quarters[i], b), sub)], preferred_element_type=f32)
            value = pf[i] + jnp.concatenate(
                [jnp.where(is_gate, term, 0.0), jnp.where(is_gate, 0.0, term)], axis=1)
            if i == 1:
                fwd[b] = value
            elif i == 3:
                own[b] = value
            else:
                s1_send[i // 2, b] = value.astype(bf16)
                s1_copy(i // 2, b).start()

        @pl.when(b < 3)
        def _():
            fill(b + 1)

        @pl.when(b > 0)
        def _():
            pass_on(b - 1)

        @pl.when(b > 1)
        def _():
            finish(b - 2, 0)

        return carry

    lax.fori_loop(0, 4, spread, 0)
    pass_on(jnp.int32(3))
    finish(jnp.int32(2), 0)
    finish(jnp.int32(3), 0)

    down_low = jnp.zeros((16, total), f32)
    for a in range(16):
        down_low = down_low + jnp.where(slot_row == a, dinner[a * 16:(a + 1) * 16, :], 0.0)
    dx_send[...] = down_low
    dx_recv[me] = down_low

    def dx_copy(owner, e, peer):
        return remote(dx_send, dx_recv.at[owner], dx_ss.at[e], dx_rs.at[owner], peer // 4, lax.rem(peer, 4))

    def dx_start(e, carry):
        dx_copy(me, e, lax.rem(me + e, 16)).start()
        return carry

    lax.fori_loop(1, 16, dx_start, 0)
    add_others(jnp.int32(3))

    def dx_wait(e, carry):
        peer = lax.rem(me + e, 16)
        dx_copy(peer, e, peer).wait_recv()
        dx_copy(peer, e, peer).wait_send()
        return carry

    lax.fori_loop(1, 16, dx_wait, 0)
    down_low = dx_recv[0]
    for e in range(1, 16):
        down_low = down_low + dx_recv[e]
    placed_down = jnp.concatenate(
        [jnp.where(slot_row == me_w * 4 + a, down_low, 0.0) for a in range(4)], axis=0).astype(bf16)
    small_copy(3).wait()
    acc[...] += lax.dot_general(placed_down, dout[...], TN, preferred_element_type=f32)

    def o_copy(d, dev):
        return remote(o_send.at[d - 1], o_recv.at[d - 1], o_ss.at[d - 1], o_rs.at[d - 1], dev, z)

    for d in (2, 3, 1):
        peer = lax.rem(me_w + d, 4)
        o_send[d - 1] = acc[pl.ds(pl.multiple_of(peer * rows, rows), rows), :].astype(bf16)
        o_copy(d, peer).start()
    result = stream_ref[...].astype(f32) + acc[pl.ds(pl.multiple_of(me_w * rows, rows), rows), :]
    for d in (1, 2, 3):
        o_copy(d, lax.rem(me_w + d, 4)).wait_recv()
        result = result + o_recv[d - 1].astype(f32)
    out_ref[...] = result.astype(bf16)

    for d in (1, 2, 3):
        peer = lax.rem(me_w + d, 4)
        raw_copy(me_w, d, peer).wait_send()
        o_copy(d, peer).wait_send()

    def drain(b, carry):
        s1_copy(0, b).wait_send()
        s1_copy(1, b).wait_send()
        s2_copy(b).wait_send()
        for d in (1, 2, 3):
            h_copy(z, b, d, quarters[3 - d]).wait_send()
        return carry

    lax.fori_loop(0, 4, drain, 0)


def feed_forward(stream, norm_gain, gate, up, down, ain, omaps, dai, dout, request, storage):
    rows, width = stream.shape
    total = 4 * rows
    hidden = gate.shape[1]
    sub = hidden // 16
    owned, _, rank2 = ain.shape
    f32, bf16 = jnp.float32, jnp.bfloat16
    ain_t = jnp.transpose(ain, (0, 2, 1)).reshape(owned * rank2, width)
    omap = omaps.reshape(omaps.shape[0] * omaps.shape[1], hidden)
    dai2 = dai.reshape(dai.shape[0] * dai.shape[1], dai.shape[2])
    dout2 = dout.reshape(dout.shape[0] * dout.shape[1], width)
    dma = pltpu.SemaphoreType.DMA
    vmem = pl.BlockSpec(memory_space=pltpu.VMEM)
    hbm = pl.BlockSpec(memory_space=pl.ANY)
    return pl.pallas_call(
        feed_forward_kernel,
        out_shape=jax.ShapeDtypeStruct((rows, width), bf16),
        in_specs=[pl.BlockSpec(memory_space=pltpu.SMEM)] + [vmem] * 3 + [hbm] * 7,
        out_specs=vmem,
        scratch_shapes=[
            pltpu.VMEM((4, rows, width), bf16),
            pltpu.VMEM((total, width), bf16),
            pltpu.VMEM(ain_t.shape, bf16),
            pltpu.VMEM(omap.shape, bf16),
            pltpu.VMEM(dai2.shape, bf16),
            pltpu.VMEM(dout2.shape, bf16),
            pltpu.VMEM((8, width, 2 * sub), bf16),
            pltpu.VMEM((16, sub, width), bf16),
            pltpu.VMEM((4, 16, total), f32),
            pltpu.VMEM((16, 16, total), f32),
            pltpu.VMEM((4, total, 2 * sub), f32),
            pltpu.VMEM((2, 4, total, 2 * sub), bf16),
            pltpu.VMEM((2, 4, total, 2 * sub), bf16),
            pltpu.VMEM((4, total, 2 * sub), f32),
            pltpu.VMEM((4, total, 2 * sub), f32),
            pltpu.VMEM((4, total, 2 * sub), bf16),
            pltpu.VMEM((4, total, 2 * sub), bf16),
            pltpu.VMEM((4, 4, total, sub), bf16),
            pltpu.VMEM((dai2.shape[0], total), f32),
            pltpu.VMEM((16, total), f32),
            pltpu.VMEM((16, 16, total), f32),
            pltpu.VMEM((total, width), f32),
            pltpu.VMEM((3, rows, width), bf16),
            pltpu.VMEM((3, rows, width), bf16),
            dma((4,)), dma((8, 2)), dma((16,)),
            dma((3,)), dma((4,)), dma((16,)), dma((16,)),
            dma((2, 4)), dma((2, 4)), dma((4,)), dma((4,)),
            dma((3, 4)), dma((4, 4)), dma((16,)), dma((16,)), dma((3,)), dma((3,)),
        ],
        compiler_params=pltpu.CompilerParams(
            collective_id=0, has_side_effects=True, vmem_limit_bytes=58 * 2**20),
        cost_estimate=pl.CostEstimate(
            flops=6 * total * width * hidden, bytes_accessed=6 * width * hidden, transcendentals=0),
    )(storage, request.reshape(1, total), stream, norm_gain.reshape(1, width), ain_t, omap, dai2, dout2,
      gate, up, down)


def per_device(
    queries,
    cached_key_rows,
    cached_value_rows,
    fresh_token_key,
    fresh_token_value,
    lengths,
    residual,
    norm_gain_vector,
    gate_matrix,
    up_matrix,
    down_matrix,
    adapter_input_maps,
    adapter_output_maps,
    down_adapter_input,
    down_adapter_output,
    request_adapter,
    adapter_storage_slot,
):
    rows_here = queries.shape[0]
    kv_here = cached_key_rows.shape[1]
    context = cached_key_rows.shape[2]
    head_size = cached_key_rows.shape[3]
    group_size = queries.shape[1] // (kv_here * head_size)
    score_scale = 1.0 / math.sqrt(head_size)
    query_heads = queries.reshape(rows_here, kv_here, group_size, head_size)
    scores = (
        jnp.einsum(
            "rkgd,rkld->rkgl", query_heads, cached_key_rows, preferred_element_type=jnp.float32
        )
        * score_scale
    )
    own_score = (
        jnp.einsum(
            "rkgd,rkd->rkg",
            query_heads,
            fresh_token_key.reshape(rows_here, kv_here, head_size),
            preferred_element_type=jnp.float32,
        )
        * score_scale
    )
    visible = lax.broadcasted_iota(jnp.int32, (rows_here, context), 1) < lengths[:, None]
    scores = jnp.where(visible[:, None, None, :], scores, jnp.float32(-1e30))
    row_peak = jnp.maximum(jnp.max(scores, axis=-1), own_score)
    weights = jnp.exp(scores - row_peak[..., None])
    own_weight = jnp.exp(own_score - row_peak)
    denominator = jnp.sum(weights, axis=-1) + own_weight
    fresh_value = fresh_token_value.reshape(rows_here, kv_here, head_size).astype(jnp.float32)
    mixed = jnp.einsum(
        "rkgl,rkld->rkgd",
        weights.astype(jnp.bfloat16),
        cached_value_rows,
        preferred_element_type=jnp.float32,
    )
    mixed = mixed + own_weight[..., None] * fresh_value[:, :, None, :]
    attn = (mixed / denominator[..., None]).reshape(rows_here, -1).astype(jnp.bfloat16)
    stream = (residual.astype(jnp.float32) + attn.astype(jnp.float32)).astype(jnp.bfloat16)
    if lax.axis_size("tp") == 4 and lax.axis_size("wide") == 4 and rows_here == 32:
        return feed_forward(
            stream,
            norm_gain_vector,
            gate_matrix,
            up_matrix,
            down_matrix,
            adapter_input_maps,
            adapter_output_maps,
            down_adapter_input,
            down_adapter_output,
            request_adapter,
            adapter_storage_slot,
        )
    tp_count = lax.axis_size("tp")
    my_tp = lax.axis_index("tp")
    my_wide = lax.axis_index("wide")
    width_portion = residual.shape[1]
    as_float = stream.astype(jnp.float32)
    square_sum = lax.psum(jnp.sum(as_float * as_float, axis=1, keepdims=True), "tp")
    mean_square = square_sum / jnp.float32(width_portion * tp_count)
    normed = (
        as_float * lax.rsqrt(mean_square + 1e-05) * norm_gain_vector.astype(jnp.float32)[None, :]
    ).astype(jnp.bfloat16)
    owned_number = adapter_input_maps.shape[0]
    adapter_number = adapter_output_maps.shape[0]
    rank_portion = adapter_output_maps.shape[1]
    adapter_rank_size = down_adapter_input.shape[1]
    hidden_portion = gate_matrix.shape[1]
    subset_width = down_adapter_input.shape[2]
    every_request_row = request_adapter.shape[0]
    adapter_ids = lax.broadcasted_iota(jnp.int32, (every_request_row, adapter_number), 1)
    adapter_hits = request_adapter[:, None] == adapter_ids
    slot_of_row = jnp.sum(jnp.where(adapter_hits, adapter_storage_slot[None, :], 0), axis=1)
    slot_hits = slot_of_row[:, None] == adapter_ids
    owned_ids = my_wide * owned_number + lax.broadcasted_iota(
        jnp.int32, (every_request_row, owned_number), 1
    )
    local_hits = slot_of_row[:, None] == owned_ids
    inner_lookup = jnp.transpose(adapter_input_maps, (1, 0, 2)).reshape(
        width_portion, owned_number * 2 * adapter_rank_size
    )
    block_rows = lax.all_gather(normed, "wide", axis=0, tiled=True)
    request_number = block_rows.shape[0]
    gate_part = jnp.dot(block_rows, gate_matrix, preferred_element_type=jnp.float32)
    up_part = jnp.dot(block_rows, up_matrix, preferred_element_type=jnp.float32)
    inner_all = jnp.dot(block_rows, inner_lookup, preferred_element_type=jnp.float32).reshape(
        request_number, owned_number, 2 * adapter_rank_size
    )
    inner_part = jnp.sum(jnp.where(local_hits[:, :, None], inner_all, jnp.float32(0.0)), axis=1)
    joined = jnp.concatenate([gate_part, up_part, inner_part], axis=1)
    inner_sum = lax.psum(joined[:, 2 * hidden_portion :], ("wide", "tp"))
    inner_low = inner_sum.astype(jnp.bfloat16)
    positioned = jnp.where(slot_hits[:, :, None], inner_low[:, None, :], jnp.bfloat16(0.0))
    rank_start = my_tp * rank_portion
    placed_slice = lax.dynamic_slice_in_dim(positioned, rank_start, rank_portion, 2)
    rank_position = rank_start + lax.broadcasted_iota(jnp.int32, (rank_portion,), 0)
    gate_select_mask = rank_position < adapter_rank_size
    gate_input = jnp.where(
        gate_select_mask[None, None, :], placed_slice, jnp.bfloat16(0.0)
    ).reshape(every_request_row, adapter_number * rank_portion)
    up_input = jnp.where(gate_select_mask[None, None, :], jnp.bfloat16(0.0), placed_slice).reshape(
        every_request_row, adapter_number * rank_portion
    )
    output_lookup = adapter_output_maps.reshape(adapter_number * rank_portion, hidden_portion)
    gate_pre = joined[:, :hidden_portion] + jnp.dot(
        gate_input, output_lookup, preferred_element_type=jnp.float32
    )
    up_pre = joined[:, hidden_portion : 2 * hidden_portion] + jnp.dot(
        up_input, output_lookup, preferred_element_type=jnp.float32
    )
    gate_total, up_total = lax.psum((gate_pre, up_pre), "tp")
    hidden_state = (jax.nn.silu(gate_total) * up_total).astype(jnp.bfloat16)
    hidden_subset = lax.dynamic_slice_in_dim(hidden_state, my_tp * subset_width, subset_width, 1)
    down_gathered = lax.dot_general(
        hidden_subset,
        down_adapter_input,
        (((1,), (2,)), ((), ())),
        preferred_element_type=jnp.float32,
    )
    down_part = jnp.sum(jnp.where(slot_hits[:, :, None], down_gathered, jnp.float32(0.0)), axis=1)
    down_low = lax.psum(down_part, ("wide", "tp")).astype(jnp.bfloat16)
    local_positioned = jnp.where(local_hits[:, :, None], down_low[:, None, :], jnp.bfloat16(0.0))
    adapter_change = jnp.dot(
        local_positioned.reshape(every_request_row, owned_number * adapter_rank_size),
        down_adapter_output.reshape(owned_number * adapter_rank_size, width_portion),
        preferred_element_type=jnp.float32,
    )
    product = jnp.dot(hidden_state, down_matrix, preferred_element_type=jnp.float32)
    projected = lax.psum_scatter(product, "wide", scatter_dimension=0, tiled=True)
    projected = projected + lax.psum_scatter(
        adapter_change, "wide", scatter_dimension=0, tiled=True
    )
    return (stream.astype(jnp.float32) + projected).astype(jnp.bfloat16)


def solution(mesh):
    return jax.shard_map(
        per_device,
        mesh=mesh,
        in_specs=(
            P(("groups", "wide"), "tp"),
            P(("groups", "wide"), "tp", None, None),
            P(("groups", "wide"), "tp", None, None),
            P(("groups", "wide"), "tp"),
            P(("groups", "wide"), "tp"),
            P(("groups", "wide")),
            P(("groups", "wide"), "tp"),
            P("tp"),
            P("tp", "wide"),
            P("tp", "wide"),
            P("wide", "tp"),
            P(("groups", "wide"), "tp", None),
            P("groups", "tp", "wide"),
            P("groups", None, ("wide", "tp")),
            P(("groups", "wide"), None, "tp"),
            P("groups"),
            P("groups"),
        ),
        out_specs=P(("groups", "wide"), "tp"),
        check_vma=False,
    )
```

```python
import math

import jax
import jax.numpy as jnp
from jax import lax
from jax.experimental import pallas as pl
from jax.experimental.pallas import tpu as pltpu
from jax.sharding import PartitionSpec as P

MESH = pl.DeviceIdType.MESH
NT = (((1,), (1,)), ((), ()))
TN = (((0,), (0,)), ((), ()))


def feed_forward_kernel(
    storage_ref, request_ref, stream_ref, gain_ref, ain_hbm, omap_hbm, dai_hbm, dout_hbm, gate_hbm, up_hbm, down_hbm,
    out_ref,
    raw, squares, x, ain, omap, dai, dout, w, dw,
    ex_send, ex_recv, pf, s1_send, s1_recv, fwd, own, s2_send, s2_recv,
    hid, dinner, dx_send, dx_recv, acc, o_send, o_recv,
    small_sem, w_sem, dw_sem,
    raw_ss, raw_rs, ex_ss, ex_rs, s1_ss, s1_rs, s2_ss, s2_rs, h_ss, h_rs, dx_ss, dx_rs, o_ss, o_rs,
):
    f32, bf16 = jnp.float32, jnp.bfloat16
    rows, width = stream_ref.shape
    total = 4 * rows
    sub = w.shape[2] // 2
    me_w, z = lax.axis_index("wide"), lax.axis_index("tp")
    me = me_w * 4 + z
    z1 = z + 1 - 2 * lax.rem(z, 2)
    z2 = lax.rem(z + 2, 4)
    z3 = 3 - z
    quarters = (z3, z2, z1, z)

    def column(q, b):
        return pl.multiple_of((q * 4 + b) * sub, sub)

    def w_copy(slot, b, i, start):
        half, parts = slot * 4 + i, []
        for j, src in enumerate((gate_hbm, up_hbm)):
            parts.append(pltpu.make_async_copy(
                src.at[:, pl.ds(column(quarters[i], b), sub)],
                w.at[half, :, pl.ds(j * sub, sub)], w_sem.at[half, j]))
        for part in parts:
            part.start() if start else part.wait()

    def dw_copy(k):
        return pltpu.make_async_copy(
            down_hbm.at[pl.ds(pl.multiple_of(k * sub, sub), sub), :], dw.at[k], dw_sem.at[k])

    def small_copy(j):
        src, dst = ((ain_hbm, ain), (omap_hbm, omap), (dai_hbm, dai), (dout_hbm, dout))[j]
        return pltpu.make_async_copy(src, dst, small_sem.at[j])

    def remote(src, dst, ss, rs, dev_w, dev_t):
        return pltpu.make_async_remote_copy(
            src_ref=src, dst_ref=dst, send_sem=ss, recv_sem=rs,
            device_id={"wide": dev_w, "tp": dev_t}, device_id_type=MESH)

    barrier = pltpu.get_barrier_semaphore()

    def greet(e, carry):
        peer = lax.rem(me + e, 16)
        pl.semaphore_signal(barrier, inc=1, device_id={"wide": peer // 4, "tp": lax.rem(peer, 4)},
                            device_id_type=MESH)
        return carry

    lax.fori_loop(1, 16, greet, 0)
    small_copy(0).start()
    for slot in range(2):
        for i in range(4):
            w_copy(slot, slot, i, True)
        if slot == 0:
            small_copy(1).start()
    small_copy(2).start()
    small_copy(3).start()
    raw[me_w] = stream_ref[...]
    pl.semaphore_wait(barrier, 15)

    def raw_copy(owner, d, dev):
        return remote(raw.at[owner], raw.at[owner], raw_ss.at[d - 1], raw_rs.at[owner], dev, z)

    across = lax.rem(me_w + 2, 4)
    sibling = me_w + 1 - 2 * lax.rem(me_w, 2)
    raw_copy(me_w, 1, across).start()
    raw_copy(me_w, 2, sibling).start()

    def dw_start(k, carry):
        dw_copy(k).start()
        return carry

    lax.fori_loop(0, 16, dw_start, 0)
    gain = gain_ref[...].astype(f32)

    def prepare(p):
        part = raw[p].astype(f32)
        here = pl.ds(pl.multiple_of(p * rows, rows), rows)
        squares[here, :] = jnp.broadcast_to(jnp.sum(part * part, axis=1, keepdims=True), (rows, total))
        x[here, :] = (part * gain).astype(bf16)

    prepare(me_w)
    raw_copy(across, 1, across).wait_recv()
    raw_copy(across, 3, sibling).start()
    raw_copy(sibling, 2, sibling).wait_recv()
    prepare(sibling)
    prepare(across)
    diagonal = lax.rem(sibling + 2, 4)
    raw_copy(diagonal, 3, sibling).wait_recv()
    prepare(diagonal)
    square = squares[...].T

    slot_row = jnp.zeros((1, total), jnp.int32)
    for a in range(16):
        slot_row = slot_row + jnp.where(request_ref[...] == a, storage_ref[a], 0)
    small_copy(0).wait()
    inner = lax.dot_general(ain[...], x[...], NT, preferred_element_type=f32)
    chosen = jnp.zeros((32, total), f32)
    for a in range(4):
        chosen = chosen + jnp.where(slot_row == me_w * 4 + a, inner[a * 32:(a + 1) * 32], 0.0)
    for t in range(4):
        ex_send[t, 0:8, :] = chosen[t * 8:(t + 1) * 8]
        ex_send[t, 8:16, :] = square[0:8]

    def ex_start(e, carry):
        peer = lax.rem(me + e, 16)
        pt = lax.rem(peer, 4)
        remote(ex_send.at[pt], ex_recv.at[me], ex_ss.at[e], ex_rs.at[me], peer // 4, pt).start()
        return carry

    lax.fori_loop(1, 16, ex_start, 0)
    ex_recv[me] = ex_send[z]

    def fill(b):
        slot = lax.rem(b, 2)
        for i in range(4):
            w_copy(slot, b, i, False)
            pf[i] = jnp.dot(x[...], w[slot * 4 + i], preferred_element_type=f32)

        @pl.when(b < 2)
        def _():
            for i in range(4):
                w_copy(slot, b + 2, i, True)

    fill(jnp.int32(0))

    def ex_wait(e, carry):
        peer = lax.rem(me + e, 16)
        desc = remote(ex_send.at[z], ex_recv.at[peer], ex_ss.at[e], ex_rs.at[peer], peer // 4, lax.rem(peer, 4))
        desc.wait_recv()
        desc.wait_send()
        return carry

    lax.fori_loop(1, 16, ex_wait, 0)
    low = ex_recv[0, 0:8, :]
    for e in range(1, 16):
        low = low + ex_recv[e, 0:8, :]
    square = ex_recv[me_w * 4, 8:16, :]
    for t in range(1, 4):
        square = square + ex_recv[me_w * 4 + t, 8:16, :]
    scale_row = lax.rsqrt(square / f32(width * 4) + 1e-05)
    scale = jnp.broadcast_to(scale_row[0:1], (total, total)).T
    scale = jnp.concatenate([scale] * (sub // total), axis=1)
    placed = jnp.concatenate([jnp.where(slot_row == a, low, 0.0) for a in range(16)], axis=0).T.astype(bf16)
    is_gate = z < 2
    small_copy(1).wait()

    def s1_copy(j, b):
        return remote(s1_send.at[j, b], s1_recv.at[j, b], s1_ss.at[j, b], s1_rs.at[j, b], me_w, z1)

    def s2_copy(b):
        return remote(s2_send.at[b], s2_recv.at[b], s2_ss.at[b], s2_rs.at[b], me_w, z2)

    def pass_on(b):
        s1_copy(0, b).wait_recv()
        s2_send[b] = (fwd[b] + s1_recv[0, b].astype(f32)).astype(bf16)
        s2_copy(b).start()

    def h_copy(q, b, d, dev):
        return remote(hid.at[q, b], hid.at[q, b], h_ss.at[d - 1, b], h_rs.at[q, b], me_w, dev)

    def add_product(q, b):
        k = q * 4 + b
        dw_copy(k).wait()
        acc[...] += jnp.dot(hid[q, b], dw[k], preferred_element_type=f32)

    def add_others(b):
        for d in (1, 2, 3):
            q = quarters[3 - d]
            h_copy(q, b, d, q).wait_recv()
            add_product(q, b)

    acc[...] = jnp.zeros_like(acc)
    dinner[...] = jnp.zeros_like(dinner)
    small_copy(2).wait()

    def dx_copy(owner, e, peer):
        return remote(dx_send, dx_recv.at[owner], dx_ss.at[e], dx_rs.at[owner], peer // 4, lax.rem(peer, 4))

    def dx_start(e, carry):
        dx_copy(me, e, lax.rem(me + e, 16)).start()
        return carry

    def send_low():
        down_low = jnp.zeros((16, total), f32)
        for a in range(16):
            down_low = down_low + jnp.where(slot_row == a, dinner[a * 16:(a + 1) * 16, :], 0.0)
        dx_send[...] = down_low
        dx_recv[me] = down_low
        lax.fori_loop(1, 16, dx_start, 0)

    def finish(b, last):
        s1_copy(1, b).wait_recv()
        s2_copy(b).wait_recv()
        value = own[b] + s1_recv[1, b].astype(f32) + s2_recv[b].astype(f32)
        gate = value[:, :sub] * scale
        up = value[:, sub:] * scale
        hid[z, b] = (gate / (1.0 + jnp.exp(-gate)) * up).astype(bf16)
        for d in (3, 2, 1):
            h_copy(z, b, d, quarters[3 - d]).start()
        dinner[...] += lax.dot_general(
            dai[:, pl.ds(pl.multiple_of(b * sub, sub), sub)], hid[z, b], NT, preferred_element_type=f32)
        if last:
            send_low()
        add_product(z, b)

        @pl.when(b > 0)
        def _():
            add_others(b - 1)


    def spread(b, carry):
        for i in range(4):
            term = jnp.dot(placed, omap[:, pl.ds(column(quarters[i], b), sub)], preferred_element_type=f32)
            value = pf[i] + jnp.concatenate(
                [jnp.where(is_gate, term, 0.0), jnp.where(is_gate, 0.0, term)], axis=1)
            if i == 1:
                fwd[b] = value
            elif i == 3:
                own[b] = value
            else:
                s1_send[i // 2, b] = value.astype(bf16)
                s1_copy(i // 2, b).start()

        @pl.when(b < 3)
        def _():
            fill(b + 1)

        @pl.when(b > 0)
        def _():
            pass_on(b - 1)

        @pl.when(b > 1)
        def _():
            finish(b - 2, False)

        return carry

    lax.fori_loop(0, 4, spread, 0)
    pass_on(jnp.int32(3))
    finish(jnp.int32(2), False)
    finish(jnp.int32(3), True)

    add_others(jnp.int32(3))

    def dx_wait(e, carry):
        peer = lax.rem(me + e, 16)
        dx_copy(peer, e, peer).wait_recv()
        dx_copy(peer, e, peer).wait_send()
        return carry

    lax.fori_loop(1, 16, dx_wait, 0)
    down_low = dx_recv[0]
    for e in range(1, 16):
        down_low = down_low + dx_recv[e]
    placed_down = jnp.concatenate(
        [jnp.where(slot_row == me_w * 4 + a, down_low, 0.0) for a in range(4)], axis=0).astype(bf16)
    small_copy(3).wait()
    acc[...] += lax.dot_general(placed_down, dout[...], TN, preferred_element_type=f32)

    def o_copy(d, dev):
        return remote(o_send.at[d - 1], o_recv.at[d - 1], o_ss.at[d - 1], o_rs.at[d - 1], dev, z)

    for d in (2, 3, 1):
        peer = lax.rem(me_w + d, 4)
        o_send[d - 1] = acc[pl.ds(pl.multiple_of(peer * rows, rows), rows), :].astype(bf16)
        o_copy(d, peer).start()
    result = stream_ref[...].astype(f32) + acc[pl.ds(pl.multiple_of(me_w * rows, rows), rows), :]
    for d in (1, 2, 3):
        o_copy(d, lax.rem(me_w + d, 4)).wait_recv()
        result = result + o_recv[d - 1].astype(f32)
    out_ref[...] = result.astype(bf16)

    for d in (1, 2, 3):
        peer = lax.rem(me_w + d, 4)
        raw_copy(me_w, d, peer).wait_send()
        o_copy(d, peer).wait_send()

    def drain(b, carry):
        s1_copy(0, b).wait_send()
        s1_copy(1, b).wait_send()
        s2_copy(b).wait_send()
        for d in (1, 2, 3):
            h_copy(z, b, d, quarters[3 - d]).wait_send()
        return carry

    lax.fori_loop(0, 4, drain, 0)


def feed_forward(stream, norm_gain, gate, up, down, ain, omaps, dai, dout, request, storage):
    rows, width = stream.shape
    total = 4 * rows
    hidden = gate.shape[1]
    sub = hidden // 16
    owned, _, rank2 = ain.shape
    f32, bf16 = jnp.float32, jnp.bfloat16
    ain_t = jnp.transpose(ain, (0, 2, 1)).reshape(owned * rank2, width)
    omap = omaps.reshape(omaps.shape[0] * omaps.shape[1], hidden)
    dai2 = dai.reshape(dai.shape[0] * dai.shape[1], dai.shape[2])
    dout2 = dout.reshape(dout.shape[0] * dout.shape[1], width)
    dma = pltpu.SemaphoreType.DMA
    vmem = pl.BlockSpec(memory_space=pltpu.VMEM)
    hbm = pl.BlockSpec(memory_space=pl.ANY)
    return pl.pallas_call(
        feed_forward_kernel,
        out_shape=jax.ShapeDtypeStruct((rows, width), bf16),
        in_specs=[pl.BlockSpec(memory_space=pltpu.SMEM)] + [vmem] * 3 + [hbm] * 7,
        out_specs=vmem,
        scratch_shapes=[
            pltpu.VMEM((4, rows, width), bf16),
            pltpu.VMEM((total, total), f32),
            pltpu.VMEM((total, width), bf16),
            pltpu.VMEM(ain_t.shape, bf16),
            pltpu.VMEM(omap.shape, bf16),
            pltpu.VMEM(dai2.shape, bf16),
            pltpu.VMEM(dout2.shape, bf16),
            pltpu.VMEM((8, width, 2 * sub), bf16),
            pltpu.VMEM((16, sub, width), bf16),
            pltpu.VMEM((4, 16, total), f32),
            pltpu.VMEM((16, 16, total), f32),
            pltpu.VMEM((4, total, 2 * sub), f32),
            pltpu.VMEM((2, 4, total, 2 * sub), bf16),
            pltpu.VMEM((2, 4, total, 2 * sub), bf16),
            pltpu.VMEM((4, total, 2 * sub), f32),
            pltpu.VMEM((4, total, 2 * sub), f32),
            pltpu.VMEM((4, total, 2 * sub), bf16),
            pltpu.VMEM((4, total, 2 * sub), bf16),
            pltpu.VMEM((4, 4, total, sub), bf16),
            pltpu.VMEM((dai2.shape[0], total), f32),
            pltpu.VMEM((16, total), f32),
            pltpu.VMEM((16, 16, total), f32),
            pltpu.VMEM((total, width), f32),
            pltpu.VMEM((3, rows, width), bf16),
            pltpu.VMEM((3, rows, width), bf16),
            dma((4,)), dma((8, 2)), dma((16,)),
            dma((3,)), dma((4,)), dma((16,)), dma((16,)),
            dma((2, 4)), dma((2, 4)), dma((4,)), dma((4,)),
            dma((3, 4)), dma((4, 4)), dma((16,)), dma((16,)), dma((3,)), dma((3,)),
        ],
        compiler_params=pltpu.CompilerParams(
            collective_id=0, has_side_effects=True, vmem_limit_bytes=58 * 2**20),
        cost_estimate=pl.CostEstimate(
            flops=6 * total * width * hidden, bytes_accessed=6 * width * hidden, transcendentals=0),
    )(storage, request.reshape(1, total), stream, norm_gain.reshape(1, width), ain_t, omap, dai2, dout2,
      gate, up, down)


def per_device(
    queries,
    cached_key_rows,
    cached_value_rows,
    fresh_token_key,
    fresh_token_value,
    lengths,
    residual,
    norm_gain_vector,
    gate_matrix,
    up_matrix,
    down_matrix,
    adapter_input_maps,
    adapter_output_maps,
    down_adapter_input,
    down_adapter_output,
    request_adapter,
    adapter_storage_slot,
):
    rows_here = queries.shape[0]
    kv_here = cached_key_rows.shape[1]
    context = cached_key_rows.shape[2]
    head_size = cached_key_rows.shape[3]
    group_size = queries.shape[1] // (kv_here * head_size)
    score_scale = 1.0 / math.sqrt(head_size)
    query_heads = queries.reshape(rows_here, kv_here, group_size, head_size)
    scores = (
        jnp.einsum(
            "rkgd,rkld->rkgl", query_heads, cached_key_rows, preferred_element_type=jnp.float32
        )
        * score_scale
    )
    own_score = (
        jnp.einsum(
            "rkgd,rkd->rkg",
            query_heads,
            fresh_token_key.reshape(rows_here, kv_here, head_size),
            preferred_element_type=jnp.float32,
        )
        * score_scale
    )
    visible = lax.broadcasted_iota(jnp.int32, (rows_here, context), 1) < lengths[:, None]
    scores = jnp.where(visible[:, None, None, :], scores, jnp.float32(-1e30))
    row_peak = jnp.maximum(jnp.max(scores, axis=-1), own_score)
    weights = jnp.exp(scores - row_peak[..., None])
    own_weight = jnp.exp(own_score - row_peak)
    denominator = jnp.sum(weights, axis=-1) + own_weight
    fresh_value = fresh_token_value.reshape(rows_here, kv_here, head_size).astype(jnp.float32)
    mixed = jnp.einsum(
        "rkgl,rkld->rkgd",
        weights.astype(jnp.bfloat16),
        cached_value_rows,
        preferred_element_type=jnp.float32,
    )
    mixed = mixed + own_weight[..., None] * fresh_value[:, :, None, :]
    attn = (mixed / denominator[..., None]).reshape(rows_here, -1).astype(jnp.bfloat16)
    stream = (residual.astype(jnp.float32) + attn.astype(jnp.float32)).astype(jnp.bfloat16)
    if lax.axis_size("tp") == 4 and lax.axis_size("wide") == 4 and rows_here == 32:
        return feed_forward(
            stream,
            norm_gain_vector,
            gate_matrix,
            up_matrix,
            down_matrix,
            adapter_input_maps,
            adapter_output_maps,
            down_adapter_input,
            down_adapter_output,
            request_adapter,
            adapter_storage_slot,
        )
    tp_count = lax.axis_size("tp")
    my_tp = lax.axis_index("tp")
    my_wide = lax.axis_index("wide")
    width_portion = residual.shape[1]
    as_float = stream.astype(jnp.float32)
    square_sum = lax.psum(jnp.sum(as_float * as_float, axis=1, keepdims=True), "tp")
    mean_square = square_sum / jnp.float32(width_portion * tp_count)
    normed = (
        as_float * lax.rsqrt(mean_square + 1e-05) * norm_gain_vector.astype(jnp.float32)[None, :]
    ).astype(jnp.bfloat16)
    owned_number = adapter_input_maps.shape[0]
    adapter_number = adapter_output_maps.shape[0]
    rank_portion = adapter_output_maps.shape[1]
    adapter_rank_size = down_adapter_input.shape[1]
    hidden_portion = gate_matrix.shape[1]
    subset_width = down_adapter_input.shape[2]
    every_request_row = request_adapter.shape[0]
    adapter_ids = lax.broadcasted_iota(jnp.int32, (every_request_row, adapter_number), 1)
    adapter_hits = request_adapter[:, None] == adapter_ids
    slot_of_row = jnp.sum(jnp.where(adapter_hits, adapter_storage_slot[None, :], 0), axis=1)
    slot_hits = slot_of_row[:, None] == adapter_ids
    owned_ids = my_wide * owned_number + lax.broadcasted_iota(
        jnp.int32, (every_request_row, owned_number), 1
    )
    local_hits = slot_of_row[:, None] == owned_ids
    inner_lookup = jnp.transpose(adapter_input_maps, (1, 0, 2)).reshape(
        width_portion, owned_number * 2 * adapter_rank_size
    )
    block_rows = lax.all_gather(normed, "wide", axis=0, tiled=True)
    request_number = block_rows.shape[0]
    gate_part = jnp.dot(block_rows, gate_matrix, preferred_element_type=jnp.float32)
    up_part = jnp.dot(block_rows, up_matrix, preferred_element_type=jnp.float32)
    inner_all = jnp.dot(block_rows, inner_lookup, preferred_element_type=jnp.float32).reshape(
        request_number, owned_number, 2 * adapter_rank_size
    )
    inner_part = jnp.sum(jnp.where(local_hits[:, :, None], inner_all, jnp.float32(0.0)), axis=1)
    joined = jnp.concatenate([gate_part, up_part, inner_part], axis=1)
    inner_sum = lax.psum(joined[:, 2 * hidden_portion :], ("wide", "tp"))
    inner_low = inner_sum.astype(jnp.bfloat16)
    positioned = jnp.where(slot_hits[:, :, None], inner_low[:, None, :], jnp.bfloat16(0.0))
    rank_start = my_tp * rank_portion
    placed_slice = lax.dynamic_slice_in_dim(positioned, rank_start, rank_portion, 2)
    rank_position = rank_start + lax.broadcasted_iota(jnp.int32, (rank_portion,), 0)
    gate_select_mask = rank_position < adapter_rank_size
    gate_input = jnp.where(
        gate_select_mask[None, None, :], placed_slice, jnp.bfloat16(0.0)
    ).reshape(every_request_row, adapter_number * rank_portion)
    up_input = jnp.where(gate_select_mask[None, None, :], jnp.bfloat16(0.0), placed_slice).reshape(
        every_request_row, adapter_number * rank_portion
    )
    output_lookup = adapter_output_maps.reshape(adapter_number * rank_portion, hidden_portion)
    gate_pre = joined[:, :hidden_portion] + jnp.dot(
        gate_input, output_lookup, preferred_element_type=jnp.float32
    )
    up_pre = joined[:, hidden_portion : 2 * hidden_portion] + jnp.dot(
        up_input, output_lookup, preferred_element_type=jnp.float32
    )
    gate_total, up_total = lax.psum((gate_pre, up_pre), "tp")
    hidden_state = (jax.nn.silu(gate_total) * up_total).astype(jnp.bfloat16)
    hidden_subset = lax.dynamic_slice_in_dim(hidden_state, my_tp * subset_width, subset_width, 1)
    down_gathered = lax.dot_general(
        hidden_subset,
        down_adapter_input,
        (((1,), (2,)), ((), ())),
        preferred_element_type=jnp.float32,
    )
    down_part = jnp.sum(jnp.where(slot_hits[:, :, None], down_gathered, jnp.float32(0.0)), axis=1)
    down_low = lax.psum(down_part, ("wide", "tp")).astype(jnp.bfloat16)
    local_positioned = jnp.where(local_hits[:, :, None], down_low[:, None, :], jnp.bfloat16(0.0))
    adapter_change = jnp.dot(
        local_positioned.reshape(every_request_row, owned_number * adapter_rank_size),
        down_adapter_output.reshape(owned_number * adapter_rank_size, width_portion),
        preferred_element_type=jnp.float32,
    )
    product = jnp.dot(hidden_state, down_matrix, preferred_element_type=jnp.float32)
    projected = lax.psum_scatter(product, "wide", scatter_dimension=0, tiled=True)
    projected = projected + lax.psum_scatter(
        adapter_change, "wide", scatter_dimension=0, tiled=True
    )
    return (stream.astype(jnp.float32) + projected).astype(jnp.bfloat16)


def solution(mesh):
    return jax.shard_map(
        per_device,
        mesh=mesh,
        in_specs=(
            P(("groups", "wide"), "tp"),
            P(("groups", "wide"), "tp", None, None),
            P(("groups", "wide"), "tp", None, None),
            P(("groups", "wide"), "tp"),
            P(("groups", "wide"), "tp"),
            P(("groups", "wide")),
            P(("groups", "wide"), "tp"),
            P("tp"),
            P("tp", "wide"),
            P("tp", "wide"),
            P("wide", "tp"),
            P(("groups", "wide"), "tp", None),
            P("groups", "tp", "wide"),
            P("groups", None, ("wide", "tp")),
            P(("groups", "wide"), None, "tp"),
            P("groups"),
            P("groups"),
        ),
        out_specs=P(("groups", "wide"), "tp"),
        check_vma=False,
    )
```
